32 devices in a mesh: groups: 2 (over y), expert: 4 (over z), tensor: 2 (over x), dp: 2 (over core).
Axes of the slice: x: 2, y: 2, z: 4, core: 2. Of those that a mesh axis runs over, the one named last changes fastest.
Arguments:
- tokens: bfloat16 [128, 3072], P(('groups', 'expert', 'tensor', 'dp')), parts along dimension 0, may hold values from -6 to 6
- expert_ids: int32 [128, 4], P(('groups', 'expert', 'tensor', 'dp')), parts along dimension 0, may hold values from 0 to 7, all different within a row; in each aligned block of 4 rows (0 to 3, 4 to 7, ...) at most 3 rows name the same one
- gate_scores: float32 [128, 4], P(('groups', 'expert', 'tensor', 'dp')), parts along dimension 0, may hold values from 0.2 to 1
- gate_weight: bfloat16 [8, 3072, 6144], P('expert', 'dp', 'tensor'), may hold values from -0.109375 to 0.109375
- up_weight: bfloat16 [8, 3072, 6144], P('expert', 'dp', 'tensor'), may hold values from -0.109375 to 0.109375
- down_weight: bfloat16 [8, 6144, 3072], P('expert', 'tensor', 'dp'), may hold values from -0.078125 to 0.078125
Outputs:
- mixed: bfloat16 [128, 3072], P(('groups', 'expert', 'tensor', 'dp')), parts along dimension 0
The draws below stay inside these ranges and needn't reach their ends.
There are 2 independent parts, one for each index of `groups`. The reference program is written for one: setup_inputs(seed, part) draws one part's arguments, and reference() takes and returns one part's arrays. A program takes and returns all parts, laid end to end along the dimension named above; an argument that names none is the same for every part. Nothing has to cross between parts.
Inputs may be any that keep to these rules, and one draw needn't show every extreme that they name: `expert_ids`: each token names 4 different experts. Among the tokens of one device no expert is named by more than 3 tokens, and that bound is reached in every draw.
All inputs are finite; a program needn't handle non-finite values.
Results may differ from the reference program's by a relative error of at most 0.0058.
Values may be sent and summed in bfloat16 or wider, within the bound.
A program may use at most 128 MiB of HBM per device.

```python
import math
import jax
import jax.numpy as jnp
import numpy as np
from jax import lax

D = 3072
FF = 6144
EXPERTS = 8
TOP = 4
TOK_DEV = 4
SLOT_SPLIT = 1
FF_SLOT = 6144
CAP = 3
TOKENS = 64
N_EXPERT = 4
N_TENSOR = 2
N_DP = 2


def block_scale(own_key, dims, shards, low, top_value):
    def one(axis_at, blocks):
        heights = jax.random.uniform(jax.random.fold_in(jax.random.fold_in(own_key, 6), axis_at), (blocks,), jnp.float32, low / len(shards), top_value / len(shards))
        return jnp.repeat(jnp.exp(heights), dims[axis_at] // blocks).reshape((-1,) + (1,) * (len(dims) - axis_at - 1))

    gain = one(*shards[0])
    for cut in shards[1:]:
        gain = gain * one(*cut)
    return gain


def shared_out(own_key, own, number, rows, amount, top, reach, skew):
    sequence = jax.random.permutation(own_key, amount)
    heavy_load, usual = load_shares(amount, rows * top, reach, skew, True), load_shares(amount, rows * top, reach, skew, False)
    places = jnp.arange(amount)

    def named(tallies, turn):
        used = int((tallies > 0).sum())
        fixed = max(1, used // 4)
        shifted = fixed + (places - fixed + turn * (used - fixed)) % max(1, amount - fixed)
        return jnp.zeros((amount,), jnp.int32).at[sequence[jnp.where(places < fixed, places, shifted)]].set(jnp.asarray(tallies, jnp.int32))

    tallies = jnp.where(number % 4 == 0, named(heavy_load, number // 4), named(usual, number - number // 4 - 1))
    mixed = jax.random.permutation(jax.random.fold_in(own, 3), amount)
    giver, receiver = mixed[0:amount // 2 * 2:2], mixed[1:amount // 2 * 2:2]
    margin = jnp.minimum(tallies[giver] - 1, reach - tallies[receiver]) // 2
    margin = jnp.where((giver == sequence[0]) | (receiver == sequence[0]) | (tallies[receiver] == 0), 0, jnp.maximum(margin, 0))
    shifted = jax.random.randint(jax.random.fold_in(own, 4), (amount // 2,), 0, 1 << 20) % (margin + 1)
    tallies = tallies.at[giver].add(-shifted).at[receiver].add(shifted)
    members = jnp.searchsorted(jnp.cumsum(tallies), jnp.arange(rows * top), side="right").astype(jnp.int32)
    table = members.reshape(top, rows).T
    table = table[jax.random.permutation(jax.random.fold_in(own, 1), rows)]
    turn = jax.random.randint(jax.random.fold_in(own, 2), (rows, 1), 0, top)
    return jnp.take_along_axis(table, (jnp.arange(top)[None, :] + turn) % top, axis=1)


def load_shares(count, total, most, slope, full):
    weights = [(1 << 20) // math.isqrt(grade ** slope) + 1 for grade in range(1, count + 1)]
    largest = most if full else min(most, max(-(-total // count), total * weights[0] // sum(weights)))
    least = 1 if total - largest >= count - 1 else 0
    given, surplus = [largest] + [least] * (count - 1), total - largest - least * (count - 1)
    while surplus > 0:
        free = [i for i in range(1, count) if given[i] < largest] or [i for i in range(1, count) if given[i] < most]
        whole, budget = sum([weights[i] for i in free]), surplus
        for i in free:
            addition = min(most - given[i], max(1, budget * weights[i] // whole), surplus)
            given[i] = given[i] + addition
            surplus = surplus - addition
    return np.array(given)


def gaussian(own_key, dims, spread, limit, pieces=(), dtype=jnp.bfloat16):
    loudness = block_scale(own_key, dims, pieces, -0.22, 0.18) if pieces else 1.0
    result = jax.random.normal(own_key, dims, jnp.float32) * spread * loudness
    return jnp.minimum(jnp.maximum(result, -limit), limit).astype(dtype)


def setup_inputs(seed: int = 0, part: int = 0) -> dict:
    keys = jax.random.split(jax.random.key(seed), 7)
    part_splits = jax.random.split(jax.random.fold_in(keys[6], part), 7)
    tokens = gaussian(part_splits[0], (TOKENS, D), 1.0, 6.0, ((0, 16),))
    expert_ids_keys = jax.random.split(jax.random.fold_in(part_splits[1], 1), TOKENS // TOK_DEV)
    expert_ids_turns = jax.random.permutation(jax.random.fold_in(part_splits[1], 3), TOKENS // TOK_DEV)
    expert_ids = jax.vmap(lambda own, number: shared_out(jax.random.fold_in(part_splits[1], 2), own, number, TOK_DEV, EXPERTS, TOP, CAP, 2))(expert_ids_keys, expert_ids_turns).reshape((TOKENS, TOP))
    gate_scores = jnp.clip(jnp.exp(math.log(1.0) - 1.609438 * jax.random.uniform(part_splits[2], (TOKENS, TOP), jnp.float32) ** block_scale(part_splits[2], (TOKENS, TOP), ((0, 16),), -0.2, 0.2)), 0.2, 1.0)
    gate_weight = gaussian(keys[3], (EXPERTS * SLOT_SPLIT, D, FF_SLOT), D ** -0.5, 0.109375, ((0, 4), (1, 2), (2, 2)))
    up_weight = gaussian(keys[4], (EXPERTS * SLOT_SPLIT, D, FF_SLOT), D ** -0.5, 0.109375, ((0, 4), (1, 2), (2, 2)))
    down_weight = gaussian(keys[5], (EXPERTS * SLOT_SPLIT, FF_SLOT, D), FF ** -0.5, 0.078125, ((0, 4), (1, 2), (2, 2)))
    return {"tokens": tokens, "expert_ids": expert_ids, "gate_scores": gate_scores, "gate_weight": gate_weight, "up_weight": up_weight, "down_weight": down_weight}


def reference(tokens, expert_ids, gate_scores, gate_weight, up_weight, down_weight):
    shares = gate_scores / jnp.sum(gate_scores, axis=1, keepdims=True)
    running = jnp.zeros((TOKENS, D), jnp.float32)
    most_rows = N_EXPERT * N_TENSOR * N_DP * CAP
    for expert in range(EXPERTS):
        hit_mask = expert_ids == expert
        chosen = jnp.any(hit_mask, axis=1)
        weight = jnp.sum(jnp.where(hit_mask, shares, jnp.zeros_like(shares)), axis=1)
        ordering = jnp.argsort(jnp.where(chosen, 0, 1).astype(jnp.int32), stable=True)[:most_rows].astype(jnp.int32)
        picked_rows = tokens[ordering]
        scaling = jnp.where(chosen[ordering], weight[ordering], jnp.zeros_like(weight[ordering]))
        for sub_idx in range(SLOT_SPLIT):
            slot_idx = expert * SLOT_SPLIT + sub_idx
            gate_part = jnp.dot(picked_rows, gate_weight[slot_idx], preferred_element_type=jnp.float32)
            up_part = jnp.dot(picked_rows, up_weight[slot_idx], preferred_element_type=jnp.float32)
            hidden = (jax.nn.silu(gate_part) * up_part).astype(jnp.bfloat16)
            slot_part = jnp.dot(hidden, down_weight[slot_idx], preferred_element_type=jnp.float32).astype(jnp.bfloat16)
            slot_part = lax.optimization_barrier(slot_part).astype(jnp.float32)
            running = running.at[ordering].add(scaling[:, None] * slot_part)
    return running.astype(jnp.bfloat16)
```

```python
import functools

import jax
import jax.numpy as jnp
from jax import lax
from jax.experimental import pallas as pl
from jax.experimental.pallas import tpu as pltpu
from jax.sharding import PartitionSpec as P

EXPERTS = 8
TOP = 4
CAP = 3
LANES = 128
MESH = pl.DeviceIdType.MESH


def kernel(
    sizes, tokens, ids, scores, gate_hbm, up_hbm, down_hbm, out,
    xsend, xrecv, xrows, gate_v, up_v, down_v, own, psend, precv, hidden, shares_v, ysend, yrecv,
    gate_sem, up_sem, down_sem, xs_sem, xr_sem, ps_sem, pr_sem, ys_sem, yr_sem,
):
    n_e, n_t, n_d, slots, sub, tok, half, ff, fc, oc, ring = sizes
    nf, no = ff // fc, half // oc
    steps = slots * nf
    g, e, t, d = (lax.axis_index(name) for name in ("groups", "expert", "tensor", "dp"))
    me = (e * n_t + t) * n_d + d
    peers = []
    for de in reversed(range(n_e)):
        for dt in reversed(range(n_t)):
            for dd in reversed(range(n_d)):
                if de or dt or dd:
                    pe, pt, pd = lax.rem(e + de, n_e), lax.rem(t + dt, n_t), lax.rem(d + dd, n_d)
                    peers.append(((g, pe, pt, pd), (pe * n_t + pt) * n_d + pd, pd))
    other = (g, e, t, lax.rem(d + 1, n_d))

    def weight_copies(step):
        s, c = step // nf, step % nf
        cols = pl.ds(pl.multiple_of(c * fc, fc), fc)
        return (
            pltpu.make_async_copy(gate_hbm.at[s, :, cols], gate_v.at[step], gate_sem.at[step]),
            pltpu.make_async_copy(up_hbm.at[s, :, cols], up_v.at[step], up_sem.at[step]),
        )

    def down_copies(c):
        return [
            pltpu.make_async_copy(
                down_hbm.at[s, :, c * oc : (c + 1) * oc], down_v.at[c, s], down_sem.at[c, s]
            )
            for s in range(slots)
        ]

    def start_weights(step, _):
        for copy in weight_copies(step):
            copy.start()
        return 0

    lax.fori_loop(0, steps, start_weights, 0)
    for c in range(no):
        for copy in down_copies(c):
            copy.start()

    barrier = pltpu.get_barrier_semaphore()
    for device, _, _ in peers:
        pl.semaphore_signal(barrier, inc=1, device_id=device, device_id_type=MESH)

    score = scores[...]
    share = score / jnp.sum(score, axis=1, keepdims=True)
    lane = lax.broadcasted_iota(jnp.int32, (tok, LANES), 1)
    table = jnp.zeros((tok, LANES), jnp.float32)
    for k in range(TOP):
        table += jnp.where(lane % (LANES // 2) == ids[:, k : k + 1], share[:, k : k + 1], 0.0)
    high = table.astype(jnp.bfloat16)
    low = (table - high.astype(jnp.float32)).astype(jnp.bfloat16)
    tail = jnp.where(lane < LANES // 2, high.astype(jnp.float32), low.astype(jnp.float32)).astype(jnp.bfloat16)
    for h in range(n_d):
        xsend[h, :, :half] = tokens[:, h * half : (h + 1) * half]
        xsend[h, :, half:] = tail
    xrecv[me] = xsend[d]

    pl.semaphore_wait(barrier, len(peers))

    def token_copy(device, row, pd, at):
        return pltpu.make_async_remote_copy(
            src_ref=xsend.at[pd], dst_ref=xrecv.at[at], send_sem=xs_sem.at[row], recv_sem=xr_sem.at[at],
            device_id=device, device_id_type=MESH,
        )

    for device, row, pd in peers:
        token_copy(device, row, pd, me).start()
    for device, row, pd in peers:
        token_copy(device, row, pd, row).wait_recv()
    count = n_e * n_t * n_d
    for b in range(0, count, 2):
        pair = jnp.concatenate([xrecv[b].astype(jnp.float32), xrecv[b + 1].astype(jnp.float32)], axis=0)
        xrows[b * tok : (b + 2) * tok, :] = pair
    rows = count * tok
    lanes = lax.broadcasted_iota(jnp.int32, (rows, LANES), 1) % (LANES // 2)
    for s in range(slots):
        mine = lanes == (e * slots + s) // sub
        shares_v[s] = jnp.broadcast_to(
            jnp.sum(jnp.where(mine, xrows[:, half:], 0.0), axis=1, keepdims=True), (rows, LANES)
        )
    x = xrows[:, :half].astype(jnp.bfloat16)

    def partial_copy(step):
        slot = lax.rem(step, ring)
        return pltpu.make_async_remote_copy(
            src_ref=psend.at[slot], dst_ref=precv.at[step], send_sem=ps_sem.at[slot], recv_sem=pr_sem.at[step],
            device_id=other, device_id_type=MESH,
        )

    def project(step):
        for copy in weight_copies(step):
            copy.wait()
        slot = lax.rem(step, ring)
        for at, weight in enumerate((gate_v, up_v)):
            part = jnp.dot(x, weight[step], preferred_element_type=jnp.float32)
            own[slot, at] = part
            psend[slot, at] = part.astype(jnp.bfloat16)
        partial_copy(step).start()

    def activate(step):
        slot = lax.rem(step, ring)
        partial_copy(step).wait()
        gate = own[slot, 0] + precv[step, 0].astype(jnp.float32)
        up = own[slot, 1] + precv[step, 1].astype(jnp.float32)
        s, c = step // nf, step % nf
        hidden[s, :, pl.ds(pl.multiple_of(c * fc, fc), fc)] = (gate / (1.0 + jnp.exp(-gate)) * up).astype(
            jnp.bfloat16
        )

    project(0)

    def up_step(step, _):
        project(step)
        activate(step - 1)
        return 0

    lax.fori_loop(1, steps, up_step, 0)
    activate(steps - 1)

    def result_copy(device, row, c, at):
        return pltpu.make_async_remote_copy(
            src_ref=ysend.at[c, row], dst_ref=yrecv.at[c, at], send_sem=ys_sem.at[c, row],
            recv_sem=yr_sem.at[c, at], device_id=device, device_id_type=MESH,
        )

    for c in range(no):
        total = jnp.zeros((rows, oc), jnp.float32)
        copies = down_copies(c)
        for s in range(slots):
            copies[s].wait()
            y = jnp.dot(hidden[s], down_v[c, s], preferred_element_type=jnp.float32)
            total += shares_v[s][:, :1] * y
        for b in range(count):
            ysend[c, b] = total[b * tok : (b + 1) * tok, :].astype(jnp.bfloat16)
        for device, row, _ in peers:
            result_copy(device, row, c, me).start()
        yrecv[c, me] = ysend[c, me]
    for c in range(no):
        for device, row, _ in peers:
            result_copy(device, row, c, row).wait_recv()
        for h in range(n_d):
            total = jnp.zeros((tok, oc), jnp.float32)
            for b in range(h, count, n_d):
                total += yrecv[c, b].astype(jnp.float32)
            out[:, h * half + c * oc : h * half + (c + 1) * oc] = total.astype(jnp.bfloat16)
    for device, row, pd in peers:
        token_copy(device, row, pd, me).wait_send()
        for c in range(no):
            result_copy(device, row, c, me).wait_send()


def fused(mesh, tokens, expert_ids, gate_scores, gate_weight, up_weight, down_weight):
    n_e, n_t, n_d = (mesh.shape[name] for name in ("expert", "tensor", "dp"))
    tok, width = tokens.shape
    slots, half, ff = gate_weight.shape
    sub = n_e * slots // EXPERTS
    fc, oc, ring = 512, 512, 3
    count = n_e * n_t * n_d
    steps, no, rows = slots * ff // fc, half // oc, count * tok
    sizes = (n_e, n_t, n_d, slots, sub, tok, half, ff, fc, oc, ring)
    dma, bf16, f32 = pltpu.SemaphoreType.DMA, jnp.bfloat16, jnp.float32
    vmem, hbm = pl.BlockSpec(memory_space=pltpu.VMEM), pl.BlockSpec(memory_space=pl.ANY)
    return pl.pallas_call(
        functools.partial(kernel, sizes),
        out_shape=jax.ShapeDtypeStruct((tok, width), bf16),
        in_specs=[vmem] * 3 + [hbm] * 3,
        out_specs=vmem,
        scratch_shapes=[
            pltpu.VMEM((n_d, tok, half + LANES), bf16),
            pltpu.VMEM((count, tok, half + LANES), bf16),
            pltpu.VMEM((rows, half + LANES), f32),
            pltpu.VMEM((steps, half, fc), bf16),
            pltpu.VMEM((steps, half, fc), bf16),
            pltpu.VMEM((no, slots, ff, oc), bf16),
            pltpu.VMEM((ring, 2, rows, fc), f32),
            pltpu.VMEM((ring, 2, rows, fc), bf16),
            pltpu.VMEM((steps, 2, rows, fc), bf16),
            pltpu.VMEM((slots, rows, ff), bf16),
            pltpu.VMEM((slots, rows, LANES), f32),
            pltpu.VMEM((no, count, tok, oc), bf16),
            pltpu.VMEM((no, count, tok, oc), bf16),
            dma((steps,)),
            dma((steps,)),
            dma((no, slots)),
            dma((count,)),
            dma((count,)),
            dma((ring,)),
            dma((steps,)),
            dma((no, count)),
            dma((no, count)),
        ],
        compiler_params=pltpu.CompilerParams(
            collective_id=0, has_side_effects=True, vmem_limit_bytes=63 * 2**20
        ),
    )(tokens, expert_ids, gate_scores, gate_weight, up_weight, down_weight)


def route_tables(expert_ids, gate_scores, owners, local_count, sub_count):
    tok_count = expert_ids.shape[0]
    flat_ids = expert_ids.reshape(-1)
    onehot = (flat_ids[:, None] == jnp.arange(EXPERTS, dtype=jnp.int32)[None, :]).astype(jnp.int32)
    earlier = jnp.cumsum(onehot, axis=0) - onehot
    position = jnp.sum(earlier * onehot, axis=1)
    shares = gate_scores / jnp.sum(gate_scores, axis=1, keepdims=True)
    owner_ids = jnp.arange(owners, dtype=jnp.int32)[:, None, None]
    queue_pos = jnp.arange(CAP, dtype=jnp.int32)[None, :, None]
    local_ids = jnp.arange(local_count, dtype=jnp.int32)[None, None, :]
    target = (owner_ids * local_count + local_ids) // sub_count
    matches = (flat_ids[None, None, None, :] == target[..., None]) & (
        position[None, None, None, :] == queue_pos[..., None]
    )
    matches = matches.reshape(owners * CAP * local_count, tok_count, TOP).astype(jnp.float32)
    picker = jnp.sum(matches, axis=2)
    combine = jnp.sum(matches * shares[None, :, :], axis=2)
    return (picker, combine)


def routed(tokens, expert_ids, gate_scores, gate_weight, up_weight, down_weight):
    owners = lax.axis_size("expert")
    dp_lanes = lax.axis_size("dp")
    local_count = gate_weight.shape[0]
    sub_count = owners * local_count // EXPERTS
    model_width = tokens.shape[1]
    half_width = model_width // dp_lanes
    picker, combine = route_tables(expert_ids, gate_scores, owners, local_count, sub_count)
    outgoing = jnp.dot(
        picker.astype(jnp.bfloat16), tokens, preferred_element_type=jnp.float32
    ).astype(jnp.bfloat16)
    outgoing = outgoing.reshape(owners, CAP, local_count, model_width)
    arrived = lax.all_to_all(
        lax.all_to_all(outgoing, "expert", split_axis=0, concat_axis=0, tiled=True),
        "dp",
        split_axis=3,
        concat_axis=1,
        tiled=True,
    )
    own_rows = owners * dp_lanes * CAP
    inputs = arrived.reshape(own_rows, local_count, half_width)
    segment = lax.all_gather(inputs, "tensor", axis=0, tiled=True)
    gate_part = jnp.einsum("rld,ldf->rlf", segment, gate_weight, preferred_element_type=jnp.float32)
    up_part = jnp.einsum("rld,ldf->rlf", segment, up_weight, preferred_element_type=jnp.float32)
    partial_value = jnp.stack([gate_part, up_part], axis=2)
    summed = lax.psum(partial_value, "dp")
    hidden = (jax.nn.silu(summed[:, :, 0]) * summed[:, :, 1]).astype(jnp.bfloat16)
    result = lax.psum_scatter(
        jnp.einsum("rlf,lfd->rld", hidden, down_weight, preferred_element_type=jnp.float32),
        "tensor",
        scatter_dimension=0,
        tiled=True,
    )
    slot_out = result.astype(jnp.bfloat16).reshape(owners, dp_lanes * CAP, local_count, half_width)
    returned_rows = lax.all_to_all(
        lax.all_to_all(slot_out, "expert", split_axis=0, concat_axis=0, tiled=True),
        "dp",
        split_axis=1,
        concat_axis=3,
        tiled=True,
    )
    returned_rows = returned_rows.reshape(owners * CAP * local_count, model_width)
    mixed = jnp.dot(
        combine.T,
        returned_rows.astype(jnp.float32),
        precision=lax.Precision.HIGHEST,
        preferred_element_type=jnp.float32,
    )
    return mixed.astype(jnp.bfloat16)


def solution(mesh):
    group = mesh.shape["expert"] * mesh.shape["tensor"] * mesh.shape["dp"]
    return jax.shard_map(
        functools.partial(fused, mesh) if group <= 16 and mesh.shape["dp"] == 2 else routed,
        mesh=mesh,
        in_specs=(
            P(("groups", "expert", "tensor", "dp"), None),
            P(("groups", "expert", "tensor", "dp"), None),
            P(("groups", "expert", "tensor", "dp"), None),
            P("expert", "dp", "tensor"),
            P("expert", "dp", "tensor"),
            P("expert", "tensor", "dp"),
        ),
        out_specs=P(("groups", "expert", "tensor", "dp"), None),
        check_vma=False,
    )
```

```python
import functools

import jax
import jax.numpy as jnp
from jax import lax
from jax.experimental import pallas as pl
from jax.experimental.pallas import tpu as pltpu
from jax.sharding import PartitionSpec as P

EXPERTS = 8
TOP = 4
CAP = 3
LANES = 128
MESH = pl.DeviceIdType.MESH


def kernel(
    sizes, tokens, ids, scores, gate_hbm, up_hbm, down_hbm, out,
    xsend, xother, xrecv, xrows, gate_v, up_v, down_v, own, psend, precv, hidden, shares_v, ysend, yrecv, zsend, zrecv,
    gate_sem, up_sem, down_sem, xo_sem, xs_sem, xr_sem, ps_sem, pr_sem, ys_sem, yr_sem, z_sem,
):
    n_e, n_t, n_d, slots, sub, tok, half, ff, fc, oc, ring = sizes
    nf, no = ff // fc, half // oc
    steps = slots * nf
    g, e, t, d = (lax.axis_index(name) for name in ("groups", "expert", "tensor", "dp"))
    me, chips = e * n_t + t, n_e * n_t
    peers = []
    for de in reversed(range(n_e)):
        for dt in reversed(range(n_t)):
            if de or dt:
                pe, pt = lax.rem(e + de, n_e), lax.rem(t + dt, n_t)
                peers.append(((g, pe, pt, d), pe * n_t + pt))
    od = lax.rem(d + 1, n_d)
    other = (g, e, t, od)

    def weight_copies(step):
        s, c = step // nf, step % nf
        cols = pl.ds(pl.multiple_of(c * fc, fc), fc)
        return (
            pltpu.make_async_copy(gate_hbm.at[s, :, cols], gate_v.at[step], gate_sem.at[step]),
            pltpu.make_async_copy(up_hbm.at[s, :, cols], up_v.at[step], up_sem.at[step]),
        )

    def down_copies(c):
        return [
            pltpu.make_async_copy(
                down_hbm.at[s, :, c * oc : (c + 1) * oc], down_v.at[c, s], down_sem.at[c, s]
            )
            for s in range(slots)
        ]

    def start_weights(step, _):
        for copy in weight_copies(step):
            copy.start()
        return 0

    lax.fori_loop(0, steps, start_weights, 0)
    for c in range(no):
        for copy in down_copies(c):
            copy.start()

    barrier = pltpu.get_barrier_semaphore()
    for device in [other] + [device for device, _ in peers]:
        pl.semaphore_signal(barrier, inc=1, device_id=device, device_id_type=MESH)

    score = scores[...]
    share = score / jnp.sum(score, axis=1, keepdims=True)
    lane = lax.broadcasted_iota(jnp.int32, (tok, LANES), 1)
    table = jnp.zeros((tok, LANES), jnp.float32)
    for k in range(TOP):
        table += jnp.where(lane % (LANES // 2) == ids[:, k : k + 1], share[:, k : k + 1], 0.0)
    high = table.astype(jnp.bfloat16)
    low = (table - high.astype(jnp.float32)).astype(jnp.bfloat16)
    tail = jnp.where(lane < LANES // 2, high.astype(jnp.float32), low.astype(jnp.float32)).astype(jnp.bfloat16)
    for h in range(n_d):
        xsend[h, :, :half] = tokens[:, h * half : (h + 1) * half]
        xsend[h, :, half:] = tail

    pl.semaphore_wait(barrier, len(peers) + 1)

    swap = pltpu.make_async_remote_copy(
        src_ref=xsend.at[od], dst_ref=xother, send_sem=xo_sem.at[0], recv_sem=xo_sem.at[1],
        device_id=other, device_id_type=MESH,
    )
    swap.start()
    swap.wait()
    mine, theirs = xsend[d].astype(jnp.float32), xother[...].astype(jnp.float32)
    both = jnp.concatenate([jnp.where(d == 0, mine, theirs), jnp.where(d == 0, theirs, mine)], axis=0)
    xrecv[me] = both.astype(jnp.bfloat16)

    def token_copy(device, row, at):
        return pltpu.make_async_remote_copy(
            src_ref=xrecv.at[me], dst_ref=xrecv.at[at], send_sem=xs_sem.at[row], recv_sem=xr_sem.at[at],
            device_id=device, device_id_type=MESH,
        )

    for device, row in peers:
        token_copy(device, row, me).start()
    for device, row in peers:
        token_copy(device, row, row).wait_recv()
    pair = n_d * tok
    rows = chips * pair
    for b in range(chips):
        xrows[b * pair : (b + 1) * pair, :] = xrecv[b].astype(jnp.float32)
    lanes = lax.broadcasted_iota(jnp.int32, (rows, LANES), 1) % (LANES // 2)
    for s in range(slots):
        mine = lanes == (e * slots + s) // sub
        shares_v[s] = jnp.broadcast_to(
            jnp.sum(jnp.where(mine, xrows[:, half:], 0.0), axis=1, keepdims=True), (rows, LANES)
        )
    x = xrows[:, :half].astype(jnp.bfloat16)

    def partial_copy(step):
        slot = lax.rem(step, ring)
        return pltpu.make_async_remote_copy(
            src_ref=psend.at[slot], dst_ref=precv.at[step], send_sem=ps_sem.at[slot], recv_sem=pr_sem.at[step],
            device_id=other, device_id_type=MESH,
        )

    def project(step):
        for copy in weight_copies(step):
            copy.wait()
        slot = lax.rem(step, ring)
        for at, weight in enumerate((gate_v, up_v)):
            part = jnp.dot(x, weight[step], preferred_element_type=jnp.float32)
            own[slot, at] = part
            psend[slot, at] = part.astype(jnp.bfloat16)
        partial_copy(step).start()

    def activate(step):
        slot = lax.rem(step, ring)
        partial_copy(step).wait()
        gate = own[slot, 0] + precv[step, 0].astype(jnp.float32)
        up = own[slot, 1] + precv[step, 1].astype(jnp.float32)
        s, c = step // nf, step % nf
        hidden[s, :, pl.ds(pl.multiple_of(c * fc, fc), fc)] = (gate / (1.0 + jnp.exp(-gate)) * up).astype(
            jnp.bfloat16
        )

    project(0)

    def up_step(step, _):
        project(step)
        activate(step - 1)
        return 0

    lax.fori_loop(1, steps, up_step, 0)
    activate(steps - 1)

    def result_copy(device, row, c, at):
        return pltpu.make_async_remote_copy(
            src_ref=ysend.at[c, row], dst_ref=yrecv.at[c, at], send_sem=ys_sem.at[c, row],
            recv_sem=yr_sem.at[c, at], device_id=device, device_id_type=MESH,
        )

    for c in range(no):
        total = jnp.zeros((rows, oc), jnp.float32)
        copies = down_copies(c)
        for s in range(slots):
            copies[s].wait()
            y = jnp.dot(hidden[s], down_v[c, s], preferred_element_type=jnp.float32)
            total += shares_v[s][:, :1] * y
        for b in range(chips):
            ysend[c, b] = total[b * pair : (b + 1) * pair, :].astype(jnp.bfloat16)
        for device, row in peers:
            result_copy(device, row, c, me).start()
        yrecv[c, me] = ysend[c, me]
    for c in range(no):
        for device, row in peers:
            result_copy(device, row, c, row).wait_recv()
        total = jnp.zeros((pair, oc), jnp.float32)
        for b in range(chips):
            total += yrecv[c, b].astype(jnp.float32)
        upper, lower = total[:tok], total[tok:]
        zsend[:, c * oc : (c + 1) * oc] = jnp.where(d == 0, lower, upper).astype(jnp.bfloat16)
        columns = pl.ds(pl.multiple_of(d * half + c * oc, LANES), oc)
        out[:, columns] = jnp.where(d == 0, upper, lower).astype(jnp.bfloat16)
    swap_back = pltpu.make_async_remote_copy(
        src_ref=zsend, dst_ref=zrecv, send_sem=z_sem.at[0], recv_sem=z_sem.at[1],
        device_id=other, device_id_type=MESH,
    )
    swap_back.start()
    swap_back.wait()
    out[:, pl.ds(pl.multiple_of(od * half, LANES), half)] = zrecv[...]
    for device, row in peers:
        token_copy(device, row, me).wait_send()
        for c in range(no):
            result_copy(device, row, c, me).wait_send()


def fused(mesh, tokens, expert_ids, gate_scores, gate_weight, up_weight, down_weight):
    n_e, n_t, n_d = (mesh.shape[name] for name in ("expert", "tensor", "dp"))
    tok, width = tokens.shape
    slots, half, ff = gate_weight.shape
    sub = n_e * slots // EXPERTS
    fc, oc, ring = 512, 512, 3
    count, pair = n_e * n_t, n_d * tok
    steps, no, rows = slots * ff // fc, half // oc, count * pair
    sizes = (n_e, n_t, n_d, slots, sub, tok, half, ff, fc, oc, ring)
    dma, bf16, f32 = pltpu.SemaphoreType.DMA, jnp.bfloat16, jnp.float32
    vmem, hbm = pl.BlockSpec(memory_space=pltpu.VMEM), pl.BlockSpec(memory_space=pl.ANY)
    return pl.pallas_call(
        functools.partial(kernel, sizes),
        out_shape=jax.ShapeDtypeStruct((tok, width), bf16),
        in_specs=[vmem] * 3 + [hbm] * 3,
        out_specs=vmem,
        scratch_shapes=[
            pltpu.VMEM((n_d, tok, half + LANES), bf16),
            pltpu.VMEM((tok, half + LANES), bf16),
            pltpu.VMEM((count, pair, half + LANES), bf16),
            pltpu.VMEM((rows, half + LANES), f32),
            pltpu.VMEM((steps, half, fc), bf16),
            pltpu.VMEM((steps, half, fc), bf16),
            pltpu.VMEM((no, slots, ff, oc), bf16),
            pltpu.VMEM((ring, 2, rows, fc), f32),
            pltpu.VMEM((ring, 2, rows, fc), bf16),
            pltpu.VMEM((steps, 2, rows, fc), bf16),
            pltpu.VMEM((slots, rows, ff), bf16),
            pltpu.VMEM((slots, rows, LANES), f32),
            pltpu.VMEM((no, count, pair, oc), bf16),
            pltpu.VMEM((no, count, pair, oc), bf16),
            pltpu.VMEM((tok, half), bf16),
            pltpu.VMEM((tok, half), bf16),
            dma((steps,)),
            dma((steps,)),
            dma((no, slots)),
            dma((2,)),
            dma((count,)),
            dma((count,)),
            dma((ring,)),
            dma((steps,)),
            dma((no, count)),
            dma((no, count)),
            dma((2,)),
        ],
        compiler_params=pltpu.CompilerParams(
            collective_id=0, has_side_effects=True, vmem_limit_bytes=63 * 2**20
        ),
    )(tokens, expert_ids, gate_scores, gate_weight, up_weight, down_weight)


def route_tables(expert_ids, gate_scores, owners, local_count, sub_count):
    tok_count = expert_ids.shape[0]
    flat_ids = expert_ids.reshape(-1)
    onehot = (flat_ids[:, None] == jnp.arange(EXPERTS, dtype=jnp.int32)[None, :]).astype(jnp.int32)
    earlier = jnp.cumsum(onehot, axis=0) - onehot
    position = jnp.sum(earlier * onehot, axis=1)
    shares = gate_scores / jnp.sum(gate_scores, axis=1, keepdims=True)
    owner_ids = jnp.arange(owners, dtype=jnp.int32)[:, None, None]
    queue_pos = jnp.arange(CAP, dtype=jnp.int32)[None, :, None]
    local_ids = jnp.arange(local_count, dtype=jnp.int32)[None, None, :]
    target = (owner_ids * local_count + local_ids) // sub_count
    matches = (flat_ids[None, None, None, :] == target[..., None]) & (
        position[None, None, None, :] == queue_pos[..., None]
    )
    matches = matches.reshape(owners * CAP * local_count, tok_count, TOP).astype(jnp.float32)
    picker = jnp.sum(matches, axis=2)
    combine = jnp.sum(matches * shares[None, :, :], axis=2)
    return (picker, combine)


def routed(tokens, expert_ids, gate_scores, gate_weight, up_weight, down_weight):
    owners = lax.axis_size("expert")
    dp_lanes = lax.axis_size("dp")
    local_count = gate_weight.shape[0]
    sub_count = owners * local_count // EXPERTS
    model_width = tokens.shape[1]
    half_width = model_width // dp_lanes
    picker, combine = route_tables(expert_ids, gate_scores, owners, local_count, sub_count)
    outgoing = jnp.dot(
        picker.astype(jnp.bfloat16), tokens, preferred_element_type=jnp.float32
    ).astype(jnp.bfloat16)
    outgoing = outgoing.reshape(owners, CAP, local_count, model_width)
    arrived = lax.all_to_all(
        lax.all_to_all(outgoing, "expert", split_axis=0, concat_axis=0, tiled=True),
        "dp",
        split_axis=3,
        concat_axis=1,
        tiled=True,
    )
    own_rows = owners * dp_lanes * CAP
    inputs = arrived.reshape(own_rows, local_count, half_width)
    segment = lax.all_gather(inputs, "tensor", axis=0, tiled=True)
    gate_part = jnp.einsum("rld,ldf->rlf", segment, gate_weight, preferred_element_type=jnp.float32)
    up_part = jnp.einsum("rld,ldf->rlf", segment, up_weight, preferred_element_type=jnp.float32)
    partial_value = jnp.stack([gate_part, up_part], axis=2)
    summed = lax.psum(partial_value, "dp")
    hidden = (jax.nn.silu(summed[:, :, 0]) * summed[:, :, 1]).astype(jnp.bfloat16)
    result = lax.psum_scatter(
        jnp.einsum("rlf,lfd->rld", hidden, down_weight, preferred_element_type=jnp.float32),
        "tensor",
        scatter_dimension=0,
        tiled=True,
    )
    slot_out = result.astype(jnp.bfloat16).reshape(owners, dp_lanes * CAP, local_count, half_width)
    returned_rows = lax.all_to_all(
        lax.all_to_all(slot_out, "expert", split_axis=0, concat_axis=0, tiled=True),
        "dp",
        split_axis=1,
        concat_axis=3,
        tiled=True,
    )
    returned_rows = returned_rows.reshape(owners * CAP * local_count, model_width)
    mixed = jnp.dot(
        combine.T,
        returned_rows.astype(jnp.float32),
        precision=lax.Precision.HIGHEST,
        preferred_element_type=jnp.float32,
    )
    return mixed.astype(jnp.bfloat16)


def solution(mesh):
    group = mesh.shape["expert"] * mesh.shape["tensor"] * mesh.shape["dp"]
    return jax.shard_map(
        functools.partial(fused, mesh) if group <= 16 and mesh.shape["dp"] == 2 else routed,
        mesh=mesh,
        in_specs=(
            P(("groups", "expert", "tensor", "dp"), None),
            P(("groups", "expert", "tensor", "dp"), None),
            P(("groups", "expert", "tensor", "dp"), None),
            P("expert", "dp", "tensor"),
            P("expert", "dp", "tensor"),
            P("expert", "tensor", "dp"),
        ),
        out_specs=P(("groups", "expert", "tensor", "dp"), None),
        check_vma=False,
    )
```

```python
import functools

import jax
import jax.numpy as jnp
from jax import lax
from jax.experimental import pallas as pl
from jax.experimental.pallas import tpu as pltpu
from jax.sharding import PartitionSpec as P

EXPERTS = 8
TOP = 4
CAP = 3
LANES = 128
MESH = pl.DeviceIdType.MESH


def kernel(
    sizes, tokens, ids, scores, gate_hbm, up_hbm, down_hbm, out,
    xsend, xrecv, xrows, gate_v, up_v, down_v, own, psend, precv, hidden, shares_v, ysend, yrecv,
    gate_sem, up_sem, down_sem, xs_sem, xr_sem, ps_sem, pr_sem, ys_sem, yr_sem,
):
    n_e, n_t, n_d, slots, sub, tok, half, ff, fc, oc, ring = sizes
    nf, no = ff // fc, half // oc
    steps = slots * nf
    g, e, t, d = (lax.axis_index(name) for name in ("groups", "expert", "tensor", "dp"))
    me = (e * n_t + t) * n_d + d
    peers = []
    for de in reversed(range(n_e)):
        for dt in reversed(range(n_t)):
            for dd in reversed(range(n_d)):
                if de or dt or dd:
                    pe, pt, pd = lax.rem(e + de, n_e), lax.rem(t + dt, n_t), lax.rem(d + dd, n_d)
                    peers.append(((g, pe, pt, pd), (pe * n_t + pt) * n_d + pd, pd))
    other = (g, e, t, lax.rem(d + 1, n_d))

    def weight_copies(step):
        s, c = step // nf, step % nf
        cols = pl.ds(pl.multiple_of(c * fc, fc), fc)
        return (
            pltpu.make_async_copy(gate_hbm.at[s, :, cols], gate_v.at[step], gate_sem.at[step]),
            pltpu.make_async_copy(up_hbm.at[s, :, cols], up_v.at[step], up_sem.at[step]),
        )

    def down_copies(c):
        return [
            pltpu.make_async_copy(
                down_hbm.at[s, :, c * oc : (c + 1) * oc], down_v.at[c, s], down_sem.at[c, s]
            )
            for s in range(slots)
        ]

    def start_weights(step, _):
        for copy in weight_copies(step):
            copy.start()
        return 0

    lax.fori_loop(0, steps, start_weights, 0)
    for c in range(no):
        for copy in down_copies(c):
            copy.start()

    barrier = pltpu.get_barrier_semaphore()
    for device, _, _ in peers:
        pl.semaphore_signal(barrier, inc=1, device_id=device, device_id_type=MESH)

    score = scores[...]
    share = score / jnp.sum(score, axis=1, keepdims=True)
    lane = lax.broadcasted_iota(jnp.int32, (tok, LANES), 1)
    table = jnp.zeros((tok, LANES), jnp.float32)
    for k in range(TOP):
        table += jnp.where(lane % (LANES // 2) == ids[:, k : k + 1], share[:, k : k + 1], 0.0)
    high = table.astype(jnp.bfloat16)
    low = (table - high.astype(jnp.float32)).astype(jnp.bfloat16)
    tail = jnp.where(lane < LANES // 2, high.astype(jnp.float32), low.astype(jnp.float32)).astype(jnp.bfloat16)
    for h in range(n_d):
        xsend[h, :, :half] = tokens[:, h * half : (h + 1) * half]
        xsend[h, :, half:] = tail
    xrecv[me] = xsend[d]

    pl.semaphore_wait(barrier, len(peers))

    def token_copy(device, row, pd, at):
        return pltpu.make_async_remote_copy(
            src_ref=xsend.at[pd], dst_ref=xrecv.at[at], send_sem=xs_sem.at[row], recv_sem=xr_sem.at[at],
            device_id=device, device_id_type=MESH,
        )

    for device, row, pd in peers:
        token_copy(device, row, pd, me).start()
    for device, row, pd in peers:
        token_copy(device, row, pd, row).wait_recv()
    count = n_e * n_t * n_d
    for b in range(0, count, 2):
        pair = jnp.concatenate([xrecv[b].astype(jnp.float32), xrecv[b + 1].astype(jnp.float32)], axis=0)
        xrows[b * tok : (b + 2) * tok, :] = pair
    rows = count * tok
    lanes = lax.broadcasted_iota(jnp.int32, (rows, LANES), 1) % (LANES // 2)
    for s in range(slots):
        mine = lanes == (e * slots + s) // sub
        shares_v[s] = jnp.broadcast_to(
            jnp.sum(jnp.where(mine, xrows[:, half:], 0.0), axis=1, keepdims=True), (rows, LANES)
        )
    x = xrows[:, :half].astype(jnp.bfloat16)

    def partial_copy(step):
        slot = lax.rem(step, ring)
        return pltpu.make_async_remote_copy(
            src_ref=psend.at[slot], dst_ref=precv.at[step], send_sem=ps_sem.at[slot], recv_sem=pr_sem.at[step],
            device_id=other, device_id_type=MESH,
        )

    def project(step):
        for copy in weight_copies(step):
            copy.wait()
        slot = lax.rem(step, ring)
        for at, weight in enumerate((gate_v, up_v)):
            part = jnp.dot(x, weight[step], preferred_element_type=jnp.float32)
            own[slot, at] = part
            psend[slot, at] = part.astype(jnp.bfloat16)
        partial_copy(step).start()

    def activate(step):
        slot = lax.rem(step, ring)
        partial_copy(step).wait()
        gate = own[slot, 0] + precv[step, 0].astype(jnp.float32)
        up = own[slot, 1] + precv[step, 1].astype(jnp.float32)
        s, c = step // nf, step % nf
        hidden[s, :, pl.ds(pl.multiple_of(c * fc, fc), fc)] = (gate / (1.0 + jnp.exp(-gate)) * up).astype(
            jnp.bfloat16
        )

    project(0)
    project(1)

    def up_step(step, _):
        project(step)
        activate(step - 2)
        return 0

    lax.fori_loop(2, steps, up_step, 0)
    activate(steps - 2)
    if slots == 1:
        activate(steps - 1)

    def result_copy(device, row, c, at):
        return pltpu.make_async_remote_copy(
            src_ref=ysend.at[c, row], dst_ref=yrecv.at[c, at], send_sem=ys_sem.at[c, row],
            recv_sem=yr_sem.at[c, at], device_id=device, device_id_type=MESH,
        )

    for c in range(no):
        total = jnp.zeros((rows, oc), jnp.float32)
        copies = down_copies(c)
        for s in range(slots):
            copies[s].wait()
            y = jnp.dot(hidden[s], down_v[c, s], preferred_element_type=jnp.float32)
            total += shares_v[s][:, :1] * y
            if c == 0 and s == 0 and slots > 1:
                activate(steps - 1)
        for b in range(count):
            ysend[c, b] = total[b * tok : (b + 1) * tok, :].astype(jnp.bfloat16)
        for device, row, _ in peers:
            result_copy(device, row, c, me).start()
        yrecv[c, me] = ysend[c, me]
    for c in range(no):
        for device, row, _ in peers:
            result_copy(device, row, c, row).wait_recv()
        for h in range(n_d):
            total = jnp.zeros((tok, oc), jnp.float32)
            for b in range(h, count, n_d):
                total += yrecv[c, b].astype(jnp.float32)
            out[:, h * half + c * oc : h * half + (c + 1) * oc] = total.astype(jnp.bfloat16)
    for device, row, pd in peers:
        token_copy(device, row, pd, me).wait_send()
        for c in range(no):
            result_copy(device, row, c, me).wait_send()


def fused(mesh, tokens, expert_ids, gate_scores, gate_weight, up_weight, down_weight):
    n_e, n_t, n_d = (mesh.shape[name] for name in ("expert", "tensor", "dp"))
    tok, width = tokens.shape
    slots, half, ff = gate_weight.shape
    sub = n_e * slots // EXPERTS
    fc, oc, ring = 512, 512, 3
    count = n_e * n_t * n_d
    steps, no, rows = slots * ff // fc, half // oc, count * tok
    sizes = (n_e, n_t, n_d, slots, sub, tok, half, ff, fc, oc, ring)
    dma, bf16, f32 = pltpu.SemaphoreType.DMA, jnp.bfloat16, jnp.float32
    vmem, hbm = pl.BlockSpec(memory_space=pltpu.VMEM), pl.BlockSpec(memory_space=pl.ANY)
    return pl.pallas_call(
        functools.partial(kernel, sizes),
        out_shape=jax.ShapeDtypeStruct((tok, width), bf16),
        in_specs=[vmem] * 3 + [hbm] * 3,
        out_specs=vmem,
        scratch_shapes=[
            pltpu.VMEM((n_d, tok, half + LANES), bf16),
            pltpu.VMEM((count, tok, half + LANES), bf16),
            pltpu.VMEM((rows, half + LANES), f32),
            pltpu.VMEM((steps, half, fc), bf16),
            pltpu.VMEM((steps, half, fc), bf16),
            pltpu.VMEM((no, slots, ff, oc), bf16),
            pltpu.VMEM((ring, 2, rows, fc), f32),
            pltpu.VMEM((ring, 2, rows, fc), bf16),
            pltpu.VMEM((steps, 2, rows, fc), bf16),
            pltpu.VMEM((slots, rows, ff), bf16),
            pltpu.VMEM((slots, rows, LANES), f32),
            pltpu.VMEM((no, count, tok, oc), bf16),
            pltpu.VMEM((no, count, tok, oc), bf16),
            dma((steps,)),
            dma((steps,)),
            dma((no, slots)),
            dma((count,)),
            dma((count,)),
            dma((ring,)),
            dma((steps,)),
            dma((no, count)),
            dma((no, count)),
        ],
        compiler_params=pltpu.CompilerParams(
            collective_id=0, has_side_effects=True, vmem_limit_bytes=63 * 2**20
        ),
    )(tokens, expert_ids, gate_scores, gate_weight, up_weight, down_weight)


def route_tables(expert_ids, gate_scores, owners, local_count, sub_count):
    tok_count = expert_ids.shape[0]
    flat_ids = expert_ids.reshape(-1)
    onehot = (flat_ids[:, None] == jnp.arange(EXPERTS, dtype=jnp.int32)[None, :]).astype(jnp.int32)
    earlier = jnp.cumsum(onehot, axis=0) - onehot
    position = jnp.sum(earlier * onehot, axis=1)
    shares = gate_scores / jnp.sum(gate_scores, axis=1, keepdims=True)
    owner_ids = jnp.arange(owners, dtype=jnp.int32)[:, None, None]
    queue_pos = jnp.arange(CAP, dtype=jnp.int32)[None, :, None]
    local_ids = jnp.arange(local_count, dtype=jnp.int32)[None, None, :]
    target = (owner_ids * local_count + local_ids) // sub_count
    matches = (flat_ids[None, None, None, :] == target[..., None]) & (
        position[None, None, None, :] == queue_pos[..., None]
    )
    matches = matches.reshape(owners * CAP * local_count, tok_count, TOP).astype(jnp.float32)
    picker = jnp.sum(matches, axis=2)
    combine = jnp.sum(matches * shares[None, :, :], axis=2)
    return (picker, combine)


def routed(tokens, expert_ids, gate_scores, gate_weight, up_weight, down_weight):
    owners = lax.axis_size("expert")
    dp_lanes = lax.axis_size("dp")
    local_count = gate_weight.shape[0]
    sub_count = owners * local_count // EXPERTS
    model_width = tokens.shape[1]
    half_width = model_width // dp_lanes
    picker, combine = route_tables(expert_ids, gate_scores, owners, local_count, sub_count)
    outgoing = jnp.dot(
        picker.astype(jnp.bfloat16), tokens, preferred_element_type=jnp.float32
    ).astype(jnp.bfloat16)
    outgoing = outgoing.reshape(owners, CAP, local_count, model_width)
    arrived = lax.all_to_all(
        lax.all_to_all(outgoing, "expert", split_axis=0, concat_axis=0, tiled=True),
        "dp",
        split_axis=3,
        concat_axis=1,
        tiled=True,
    )
    own_rows = owners * dp_lanes * CAP
    inputs = arrived.reshape(own_rows, local_count, half_width)
    segment = lax.all_gather(inputs, "tensor", axis=0, tiled=True)
    gate_part = jnp.einsum("rld,ldf->rlf", segment, gate_weight, preferred_element_type=jnp.float32)
    up_part = jnp.einsum("rld,ldf->rlf", segment, up_weight, preferred_element_type=jnp.float32)
    partial_value = jnp.stack([gate_part, up_part], axis=2)
    summed = lax.psum(partial_value, "dp")
    hidden = (jax.nn.silu(summed[:, :, 0]) * summed[:, :, 1]).astype(jnp.bfloat16)
    result = lax.psum_scatter(
        jnp.einsum("rlf,lfd->rld", hidden, down_weight, preferred_element_type=jnp.float32),
        "tensor",
        scatter_dimension=0,
        tiled=True,
    )
    slot_out = result.astype(jnp.bfloat16).reshape(owners, dp_lanes * CAP, local_count, half_width)
    returned_rows = lax.all_to_all(
        lax.all_to_all(slot_out, "expert", split_axis=0, concat_axis=0, tiled=True),
        "dp",
        split_axis=1,
        concat_axis=3,
        tiled=True,
    )
    returned_rows = returned_rows.reshape(owners * CAP * local_count, model_width)
    mixed = jnp.dot(
        combine.T,
        returned_rows.astype(jnp.float32),
        precision=lax.Precision.HIGHEST,
        preferred_element_type=jnp.float32,
    )
    return mixed.astype(jnp.bfloat16)


def solution(mesh):
    group = mesh.shape["expert"] * mesh.shape["tensor"] * mesh.shape["dp"]
    return jax.shard_map(
        functools.partial(fused, mesh) if group <= 16 and mesh.shape["dp"] == 2 else routed,
        mesh=mesh,
        in_specs=(
            P(("groups", "expert", "tensor", "dp"), None),
            P(("groups", "expert", "tensor", "dp"), None),
            P(("groups", "expert", "tensor", "dp"), None),
            P("expert", "dp", "tensor"),
            P("expert", "dp", "tensor"),
            P("expert", "tensor", "dp"),
        ),
        out_specs=P(("groups", "expert", "tensor", "dp"), None),
        check_vma=False,
    )
```
